128 devices in a mesh: dp: 16 (over z, y_lo, core), block: 8 (over x, y_hi).
Axes of the slice: x: 4, y: 4 (y_hi: 2, y_lo: 2; y = y_hi * 2 + y_lo), z: 4, core: 2. Of those that a mesh axis runs over, the one named last changes fastest.
Arguments:
- activations: bfloat16 [16384, 7168], P('dp', 'block'), may hold values from -6 to 6
- out_grads: bfloat16 [16384, 2112], P('dp', 'block'), may hold values from -6 to 6
- act_basis: bfloat16 [7168, 7168], P('block', 'dp'), may hold values from -0.0625 to 0.0625
- grad_basis: bfloat16 [2112, 2112], P('block', 'dp'), may hold values from -0.125 to 0.125
- query_acts: bfloat16 [512, 7168], P(None, 'block'), may hold values from -6 to 6
- query_grads: bfloat16 [512, 2112], P(None, 'block'), may hold values from -6 to 6
Outputs:
- act_cov: float32 [7168, 7168], P('dp', 'block')
- grad_cov: float32 [2112, 2112], P('dp', 'block')
- rot_act: float32 [512, 7168], P(None, 'dp')
- rot_grad: float32 [512, 2112], P(None, 'dp')
The draws below stay inside these ranges and needn't reach their ends.
All inputs are finite; a program needn't handle non-finite values.
Results may differ from the reference program's by a relative error of at most 0.0003.
Values may be sent and summed in bfloat16 or wider, within the bound.
No kernel may reach another device: no remote copies, remote signals or barrier semaphores. Data moves between devices by JAX's collectives and lax.ppermute only.
A program may use at most 192 MiB of HBM per device.

```python
import jax
import jax.numpy as jnp
from jax import lax

D_IN = 7168
D_OUT = 2112
TOKENS = 16384
QROWS = 512


def block_scale(key, shape, split, smallest, high):
    factor_of = 1.0
    for position, shards_of in split:
        draws = jax.random.uniform(jax.random.fold_in(jax.random.fold_in(key, 6), position), (shards_of,), jnp.float32, smallest / len(split), high / len(split))
        factor_of = factor_of * jnp.repeat(jnp.exp(draws), shape[position] // shards_of).reshape((-1,) + (1,) * (len(shape) - 1 - position))
    return factor_of


def normal_values(stream_key, shape, scale, reach, pieces=(), dtype=jnp.bfloat16):
    entries = scale * jax.random.normal(stream_key, shape, jnp.float32)
    if pieces:
        entries = entries * block_scale(stream_key, shape, pieces, -0.22, 0.18)
    return jnp.clip(entries, -reach, reach).astype(dtype)


def setup_inputs(seed: int = 0) -> dict:
    streams_of = jax.random.split(jax.random.key(seed), 7)
    return {
        "activations": normal_values(streams_of[0], (TOKENS, D_IN), 1.0, 6.0, ((0, 16), (1, 8))),
        "out_grads": normal_values(streams_of[1], (TOKENS, D_OUT), 1.0, 6.0, ((0, 16), (1, 8))),
        "act_basis": normal_values(streams_of[2], (D_IN, D_IN), D_IN ** -0.5, 0.0625, ((0, 8), (1, 16))),
        "grad_basis": normal_values(streams_of[3], (D_OUT, D_OUT), D_OUT ** -0.5, 0.125, ((0, 8), (1, 16))),
        "query_acts": normal_values(streams_of[4], (QROWS, D_IN), 1.0, 6.0, ((1, 8),)),
        "query_grads": normal_values(streams_of[5], (QROWS, D_OUT), 1.0, 6.0, ((1, 8),)),
    }


def reference(activations, out_grads, act_basis, grad_basis, query_acts, query_grads):
    act_wide = activations.astype(jnp.float32)
    act_cov = jnp.dot(act_wide.T, act_wide, precision=lax.Precision.HIGHEST) / TOKENS
    grad_wide = out_grads.astype(jnp.float32)
    grad_cov = jnp.dot(grad_wide.T, grad_wide, precision=lax.Precision.HIGHEST) / TOKENS
    rot_act = jnp.dot(query_acts, act_basis, preferred_element_type=jnp.float32)
    rot_grad = jnp.dot(query_grads, grad_basis, preferred_element_type=jnp.float32)
    return act_cov, grad_cov, rot_act, rot_grad
```

```python
import itertools

import jax
import jax.numpy as jnp
from jax import lax
from jax.sharding import PartitionSpec as P

AXES = ("dp", "block")
HALF = jnp.float16


def place(x, y, z, core):
    return ((z * 2 + y % 2) * 2 + core) * 8 + x * 2 + y // 2


def pairs(move):
    out = []
    for at in itertools.product(range(4), range(4), range(4), range(2)):
        x, y, z, core = move(*at)
        out.append((place(*at), place(x % 4, y % 4, z % 4, core % 2)))
    return out


SIBLING = pairs(lambda x, y, z, c: (x, y, z, c + 1))
OTHER_COLUMN = pairs(lambda x, y, z, c: (x, y + 2, z, c))
X_DOWN = pairs(lambda x, y, z, c: (x - 1, y, z, c))
X_UP = pairs(lambda x, y, z, c: (x + 1, y, z, c))
X_FAR = pairs(lambda x, y, z, c: (x + 2, y, z, c))
Z_ALONG = pairs(lambda x, y, z, c: (x, y, z + 1 - 2 * c, c))
Z_AGAINST = pairs(lambda x, y, z, c: (x, y, z - 1 + 2 * c, c))
Y_PARTNER = pairs(lambda x, y, z, c: (x, y ^ 1, z, c))
Y_MIDDLE = [p for p in pairs(lambda x, y, z, c: (x, (0, 2, 1, 3)[y], z, c)) if p[0] != p[1]]


def send(value, to):
    return lax.ppermute(value, AXES, to)


def transposed_product(left, right):
    return lax.dot_general(
        left, right, (((0,), (0,)), ((), ())), preferred_element_type=jnp.float32
    )


def covariance(own, tokens_total, where):
    x, y_hi, z, y_lo, core = where
    width = own.shape[1]
    half = width // 2

    largest = lax.pmax(jnp.max(jnp.abs(own)).astype(jnp.float32), AXES)
    largest = jnp.maximum(largest, 1e-18)
    down = 2.0 / (largest * largest)
    up = largest * largest * (0.5 / tokens_total)

    other = send(own, OTHER_COLUMN)
    sibling = send(own, SIBLING)
    other_sibling = send(other, SIBLING)

    def my_rows(block):
        return jnp.where(core == 0, block[:, :half], block[:, half:])

    rows = jnp.concatenate([my_rows(own), my_rows(sibling)], axis=0)
    rows_of = [rows, send(rows, X_DOWN), send(rows, X_FAR), send(rows, X_UP)]
    columns = jnp.concatenate(
        [
            jnp.concatenate([own, sibling], axis=0),
            jnp.concatenate([other, other_sibling], axis=0),
        ],
        axis=1,
    )
    partial = jnp.stack([transposed_product(r, columns) * down for r in rows_of])

    def toward(offset):
        return lax.dynamic_index_in_dim(partial, (z + offset - x) % 4, 0, keepdims=False)

    along = 1 - 2 * core
    first = send(toward(2).astype(HALF), Z_ALONG).astype(jnp.float32)
    third = send(toward(-along).astype(HALF), Z_AGAINST).astype(jnp.float32)
    second = send((toward(along) + first).astype(HALF), Z_ALONG).astype(jnp.float32)
    total = toward(0) + second + third

    total_own, total_other = total[:, :width], total[:, width:]
    stays = y_lo == y_hi
    near = send(jnp.where(stays, total_other, total_own).astype(HALF), Y_PARTNER)
    near = near.astype(jnp.float32)
    cross = send((total_other + near).astype(HALF), Y_MIDDLE).astype(jnp.float32)
    return jnp.where(stays, total_own + near, cross) * up


def on_device(activations, out_grads, act_basis, grad_basis, query_acts, query_grads):
    dp, block = lax.axis_index("dp"), lax.axis_index("block")
    where = (block // 2, block % 2, dp // 4, dp // 2 % 2, dp % 2)
    tokens_total = activations.shape[0] * lax.axis_size("dp")
    rot_act = lax.psum(
        jnp.dot(query_acts, act_basis, preferred_element_type=jnp.float32), "block"
    )
    rot_grad = lax.psum(
        jnp.dot(query_grads, grad_basis, preferred_element_type=jnp.float32), "block"
    )
    act_cov = covariance(activations, tokens_total, where)
    grad_cov = covariance(out_grads, tokens_total, where)
    return (act_cov, grad_cov, rot_act, rot_grad)


def solution(mesh):
    return jax.shard_map(
        on_device,
        mesh=mesh,
        in_specs=(
            P("dp", "block"),
            P("dp", "block"),
            P("block", "dp"),
            P("block", "dp"),
            P(None, "block"),
            P(None, "block"),
        ),
        out_specs=(P("dp", "block"), P("dp", "block"), P(None, "dp"), P(None, "dp")),
        check_vma=False,
    )
```

```python
import functools
import itertools

import jax
import jax.numpy as jnp
from jax import lax
from jax.experimental import pallas as pl
from jax.experimental.pallas import tpu as pltpu
from jax.sharding import PartitionSpec as P

AXES = ("dp", "block")
HALF = jnp.float16
MARK = 8


def place(x, y, z, core):
    return ((z * 2 + y % 2) * 2 + core) * 8 + x * 2 + y // 2


def pairs(move):
    out = []
    for at in itertools.product(range(4), range(4), range(4), range(2)):
        x, y, z, core = move(*at)
        out.append((place(*at), place(x % 4, y % 4, z % 4, core % 2)))
    return out


SIBLING = pairs(lambda x, y, z, c: (x, y, z, c + 1))
OTHER_COLUMN = pairs(lambda x, y, z, c: (x, y + 2, z, c))
X_FAR = pairs(lambda x, y, z, c: (x + 2, y, z, c))
X_FLIP = pairs(lambda x, y, z, c: (x ^ 1, y, z, c))
Z_ALONG = pairs(lambda x, y, z, c: (x, y, z + 1 - 2 * c, c))
Z_AGAINST = pairs(lambda x, y, z, c: (x, y, z - 1 + 2 * c, c))
X_RINGS = [
    [place(x, y, z, c) for x in range(4)]
    for y, z, c in itertools.product(range(4), range(4), range(2))
]
CHUNKS = ((0, 224), (224, 448))
Y_PARTNER = pairs(lambda x, y, z, c: (x, y ^ 1, z, c))
Y_MIDDLE = [p for p in pairs(lambda x, y, z, c: (x, (0, 2, 1, 3)[y], z, c)) if p[0] != p[1]]


def send(value, to):
    return lax.ppermute(value, AXES, to)


def turn_kernel(core, own, mine, theirs, turned):
    half = mine.shape[0]
    turned[...] = own[...].T
    mine[...] = turned[pl.ds(pl.multiple_of(core[0] * half, 16), half), :]
    theirs[...] = turned[pl.ds(pl.multiple_of((1 - core[0]) * half, 16), half), :]


def turn(own, core):
    tokens, width = own.shape
    vmem = pl.BlockSpec(memory_space=pltpu.VMEM)
    half = jax.ShapeDtypeStruct((width // 2, tokens), own.dtype)
    return pl.pallas_call(
        turn_kernel,
        out_shape=(half, half),
        in_specs=[pl.BlockSpec(memory_space=pltpu.SMEM), vmem],
        out_specs=(vmem, vmem),
        scratch_shapes=[pltpu.VMEM((width, tokens), own.dtype)],
        compiler_params=pltpu.CompilerParams(vmem_limit_bytes=24 << 20),
    )(core.reshape(1).astype(jnp.int32), own)


def product_kernel(turned, slot, rows, own, sib, oth, oth_sib, out, top, held, sem):
    blocks, _, n, _ = rows.shape
    step = pl.program_id(0)
    contract = (((1,), (1 if turned else 0,)), ((), ()))
    dot = functools.partial(
        lax.dot_general, dimension_numbers=contract, preferred_element_type=jnp.float32
    )

    @pl.when(step == 0)
    def _():
        copies = [
            pltpu.make_async_copy(
                rows.at[d],
                held.at[:, pl.ds(pl.multiple_of(slot[d] * n, 16), n), :],
                sem.at[d],
            )
            for d in range(blocks)
        ]
        for copy in copies:
            copy.start()
        for copy in copies:
            copy.wait()
        top[...] = jnp.zeros_like(top)

    def product(left, right):
        value = dot(held[0], left[...]) + dot(held[1], right[...])
        out[0] = value.reshape(out.shape[1:])
        top[...] = jnp.maximum(top[...], jnp.max(jnp.abs(value)))

    @pl.when(step == 0)
    def _():
        product(own, sib)

    @pl.when(step == 1)
    def _():
        product(oth, oth_sib)


def products(slot, rows, columns, turned=False):
    blocks, _, n, tokens = rows.shape
    width = columns[0].shape[0 if turned else 1]
    whole = pl.BlockSpec(columns[0].shape, lambda step, slot: (0, 0))
    out, top = pl.pallas_call(
        functools.partial(product_kernel, turned),
        out_shape=(
            jax.ShapeDtypeStruct((2, blocks, n, width), jnp.float32),
            jax.ShapeDtypeStruct((8, 128), jnp.float32),
        ),
        grid_spec=pltpu.PrefetchScalarGridSpec(
            num_scalar_prefetch=1,
            grid=(2,),
            in_specs=[pl.BlockSpec(memory_space=pl.ANY)] + [whole] * 4,
            out_specs=(
                pl.BlockSpec((1, blocks, n, width), lambda step, slot: (step, 0, 0, 0)),
                pl.BlockSpec((8, 128), lambda step, slot: (0, 0)),
            ),
            scratch_shapes=[
                pltpu.VMEM((2, blocks * n, tokens), rows.dtype),
                pltpu.SemaphoreType.DMA((blocks,)),
            ],
        ),
        compiler_params=pltpu.CompilerParams(vmem_limit_bytes=50 << 20),
        cost_estimate=pl.CostEstimate(
            flops=4 * blocks * n * tokens * width,
            bytes_accessed=4 * blocks * n * tokens,
            transcendentals=0,
        ),
    )(slot, rows, *columns)
    return out, jnp.clip(jnp.ceil(jnp.log2(top[0, 0])), -100.0, 100.0) - 15.0


def message(value, exponent):
    marks = value.shape[:-2] + (MARK, value.shape[-1])
    return jnp.concatenate(
        [
            (value * jnp.exp2(-exponent)).astype(HALF),
            jnp.broadcast_to(exponent, marks).astype(HALF),
        ],
        axis=-2,
    )


def read(got):
    n = got.shape[-2] - MARK
    exponent = got[..., n : n + 1, :].astype(jnp.float32)
    return got[..., :n, :].astype(jnp.float32) * jnp.exp2(exponent), exponent


def far(p):
    a = send(message(p["partial"][:, 2], p["exponent"]), Z_ALONG)
    c = send(message(p["partial"][:, 3], p["exponent"]), Z_AGAINST)
    return {**p, "a": a, "c": c}


def along(p):
    first, first_exp = read(p.pop("a"))
    exponent = jnp.maximum(first_exp, p["exponent"]) + 1.0
    return {**p, "b": send(message(p["partial"][:, 1] + first, exponent), Z_ALONG)}


def near(p):
    second, second_exp = read(p["b"])
    third, third_exp = read(p["c"])
    total = p["partial"][:, 0] + second + third
    top = jnp.maximum(jnp.maximum(second_exp, third_exp), p["exponent"]) + 2.0
    value = jnp.where(p["stays"], total[1], total[0])
    n = send(message(value, jnp.where(p["stays"], top[1], top[0])), Y_PARTNER)
    return {"total": total, "top": top, "stays": p["stays"], "n": n}


def cross(p):
    value, exponent = read(p["n"])
    exponent = jnp.maximum(p["top"][1], exponent) + 1.0
    return {**p, "m": send(message(p["total"][1] + value, exponent), Y_MIDDLE)}


def result(p):
    near, _ = read(p["n"])
    cross, _ = read(p["m"])
    return jnp.where(p["stays"], p["total"][0] + near, cross)


def halve(value, bit, to):
    rows = value.shape[0] // 2
    keep = lax.dynamic_slice_in_dim(value, bit * rows, rows, 0)
    give = lax.dynamic_slice_in_dim(value, (1 - bit) * rows, rows, 0)
    return keep + send(give, to)


def double(value, bit, to):
    got = send(value, to)
    return jnp.where(
        bit == 0,
        jnp.concatenate([value, got], axis=0),
        jnp.concatenate([got, value], axis=0),
    )


def round_x(rows):
    return lax.all_gather(rows, AXES, axis_index_groups=X_RINGS)


def on_device(activations, out_grads, act_basis, grad_basis, query_acts, query_grads):
    dp, block = lax.axis_index("dp"), lax.axis_index("block")
    x, y_hi, z, y_lo, core = block // 2, block % 2, dp // 4, dp // 2 % 2, dp % 2
    up = 1.0 / (activations.shape[0] * lax.axis_size("dp"))
    slot = jnp.stack([((d - z) * (1 - 2 * core)) % 4 for d in range(4)]).astype(jnp.int32)

    other = send(activations, OTHER_COLUMN)
    mine, theirs = turn(activations, core)
    got = send(theirs, SIBLING)
    rows = []
    for start, end in CHUNKS:
        rows.append(round_x(jnp.stack([mine[start:end], got[start:end]])))
    half = out_grads.shape[1] // 2
    grads = out_grads.T
    mine = lax.dynamic_slice_in_dim(grads, core * half, half, 0)
    theirs = lax.dynamic_slice_in_dim(grads, (1 - core) * half, half, 0)
    grad_rows = jnp.stack([mine, send(theirs, SIBLING)])
    rows.append(round_x(jnp.pad(grad_rows, ((0, 0), (0, -half % 16), (0, 0)))))
    sibling = send(activations, SIBLING)
    grad_sibling = send(grads, SIBLING)
    act_part = jnp.dot(query_acts, act_basis, preferred_element_type=jnp.float32)
    grad_part = jnp.dot(query_grads, grad_basis, preferred_element_type=jnp.float32)
    part = jnp.concatenate([act_part, grad_part], axis=1)

    rows[0], other, sibling, grad_sibling, part = lax.optimization_barrier(
        (rows[0], other, sibling, grad_sibling, part)
    )
    columns = [activations, sibling, other, send(other, SIBLING)]
    grad_other = send(grads, OTHER_COLUMN)
    grad_columns = [grads, grad_sibling, grad_other, send(grad_other, SIBLING)]

    def multiply(i):
        if i < len(CHUNKS):
            partial, exponent = products(slot, rows[i], columns)
        else:
            partial, exponent = products(slot, rows[i], grad_columns, turned=True)
            partial = partial[:, :, :half]
        return {"partial": partial, "exponent": exponent, "stays": y_lo == y_hi}

    rotate = [
        functools.partial(halve, bit=y_hi, to=OTHER_COLUMN),
        functools.partial(halve, bit=x // 2, to=X_FAR),
        functools.partial(halve, bit=x % 2, to=X_FLIP),
        functools.partial(double, bit=x % 2, to=X_FLIP),
        functools.partial(double, bit=x // 2, to=X_FAR),
        functools.partial(double, bit=y_hi, to=OTHER_COLUMN),
    ]
    steps = (far, along, near, cross)
    parts, done = [None] * len(rows), [None] * len(rows)
    for stage in range(len(rows) + len(steps)):
        for i in reversed(range(len(rows))):
            step = stage - i - 1
            if 0 <= step < len(steps):
                parts[i] = steps[step](parts[i])
        if stage < len(rotate):
            part = rotate[stage](part)
        if stage < len(rows):
            parts[stage] = multiply(stage)
        parts, part = lax.optimization_barrier((parts, part))
        i = stage - len(steps)
        if i >= 0:
            done[i] = result(parts[i]) * up
            parts[i] = None
    act_cov = jnp.concatenate(done[:-1], axis=0)
    split = act_part.shape[1]
    return (act_cov, done[-1], part[:, :split], part[:, split:])


def solution(mesh):
    return jax.shard_map(
        on_device,
        mesh=mesh,
        in_specs=(
            P("dp", "block"),
            P("dp", "block"),
            P("block", "dp"),
            P("block", "dp"),
            P(None, "block"),
            P(None, "block"),
        ),
        out_specs=(P("dp", "block"), P("dp", "block"), P(None, "dp"), P(None, "dp")),
        check_vma=False,
    )
```

```python
import functools
import itertools

import jax
import jax.numpy as jnp
from jax import lax
from jax.experimental import pallas as pl
from jax.experimental.pallas import tpu as pltpu
from jax.sharding import PartitionSpec as P

AXES = ("dp", "block")
HALF = jnp.float16


def place(x, y, z, core):
    return ((z * 2 + y % 2) * 2 + core) * 8 + x * 2 + y // 2


def pairs(move):
    out = []
    for at in itertools.product(range(4), range(4), range(4), range(2)):
        x, y, z, core = move(*at)
        out.append((place(*at), place(x % 4, y % 4, z % 4, core % 2)))
    return out


SIBLING = pairs(lambda x, y, z, c: (x, y, z, c + 1))
OTHER_COLUMN = pairs(lambda x, y, z, c: (x, y + 2, z, c))
X_DOWN = pairs(lambda x, y, z, c: (x - 1, y, z, c))
X_UP = pairs(lambda x, y, z, c: (x + 1, y, z, c))
X_FAR = pairs(lambda x, y, z, c: (x + 2, y, z, c))
X_FLIP = pairs(lambda x, y, z, c: (x ^ 1, y, z, c))
Z_ALONG = pairs(lambda x, y, z, c: (x, y, z + 1 - 2 * c, c))
Z_AGAINST = pairs(lambda x, y, z, c: (x, y, z - 1 + 2 * c, c))
X_RINGS = [
    [place(x, y, z, c) for x in range(4)]
    for y, z, c in itertools.product(range(4), range(4), range(2))
]
FIRST = 272
Y_PARTNER = pairs(lambda x, y, z, c: (x, y ^ 1, z, c))
Y_ROUND = pairs(lambda x, y, z, c: (x, (2, 0, 3, 1)[y], z, c))
Y_MIDDLE = [p for p in pairs(lambda x, y, z, c: (x, (0, 2, 1, 3)[y], z, c)) if p[0] != p[1]]


def send(value, to):
    return lax.ppermute(value, AXES, to)


def turn_kernel(core, own, mine, theirs, turned):
    half = mine.shape[0]
    turned[...] = own[...].T
    mine[...] = turned[pl.ds(pl.multiple_of(core[0] * half, 16), half), :]
    theirs[...] = turned[pl.ds(pl.multiple_of((1 - core[0]) * half, 16), half), :]


def turn(own, core):
    tokens, width = own.shape
    vmem = pl.BlockSpec(memory_space=pltpu.VMEM)
    half = jax.ShapeDtypeStruct((width // 2, tokens), own.dtype)
    return pl.pallas_call(
        turn_kernel,
        out_shape=(half, half),
        in_specs=[pl.BlockSpec(memory_space=pltpu.SMEM), vmem],
        out_specs=(vmem, vmem),
        scratch_shapes=[pltpu.VMEM((width, tokens), own.dtype)],
        compiler_params=pltpu.CompilerParams(vmem_limit_bytes=24 << 20),
    )(core.reshape(1).astype(jnp.int32), own)


def product_kernel(turned, slot, rows, own, sib, oth, oth_sib, *refs):
    *outs, held, columns, sem = refs
    tokens = held.shape[2] // 2
    block, at = pl.program_id(0), pl.program_id(1)

    def row_copy(d, half, i):
        place = held.at[i, :, pl.ds(half * tokens, tokens)]
        return pltpu.make_async_copy(rows.at[d, half], place, sem.at[half, i])

    def column_copies(i):
        copies = []
        for half, ref in enumerate(((own, sib), (oth, oth_sib))[i]):
            part = pl.ds(half * tokens, tokens)
            place = columns.at[i, :, part] if turned else columns.at[i, part, :]
            copies.append(pltpu.make_async_copy(ref, place, sem.at[half, 4 + i]))
        return copies

    @pl.when((block == 0) & (at == 0))
    def _():
        for copy in column_copies(0):
            copy.start()
        for d in range(4):
            for half in (0, 1):
                row_copy(d, half, slot[d]).start()
        for copy in column_copies(1):
            copy.start()

    for i in (0, 1):

        @pl.when((block == i) & (at == 0))
        def _(i=i):
            for copy in column_copies(i):
                copy.wait()

    for i in range(4):

        @pl.when((block == 0) & (at == i))
        def _(i=i):
            for half in (0, 1):
                row_copy(0, half, i).wait()

    for i, out in enumerate(outs):

        @pl.when(at == i)
        def _(i=i, out=out):
            out[0] = lax.dot_general(
                held[i],
                columns[block],
                (((1,), (1 if turned else 0,)), ((), ())),
                preferred_element_type=jnp.float32,
            )


def products(slot, rows, columns, turned=False):
    _, _, n, tokens = rows.shape
    width = columns[0].shape[0 if turned else 1]
    anywhere = pl.BlockSpec(memory_space=pl.ANY)
    smem = pl.BlockSpec(memory_space=pltpu.SMEM)
    held_columns = (2, width, 2 * tokens) if turned else (2, 2 * tokens, width)
    return pl.pallas_call(
        functools.partial(product_kernel, turned),
        out_shape=[jax.ShapeDtypeStruct((2, n, width), jnp.float32)] * 4,
        grid=(2, 4),
        in_specs=[smem] + [anywhere] * 5,
        out_specs=[pl.BlockSpec((1, n, width), lambda block, at: (block, 0, 0))] * 4,
        scratch_shapes=[
            pltpu.VMEM((4, n, 2 * tokens), columns[0].dtype),
            pltpu.VMEM(held_columns, columns[0].dtype),
            pltpu.SemaphoreType.DMA((2, 6)),
        ],
        compiler_params=pltpu.CompilerParams(vmem_limit_bytes=60 << 20),
        cost_estimate=pl.CostEstimate(
            flops=16 * n * tokens * width, bytes_accessed=16 * n * tokens, transcendentals=0
        ),
    )(slot, rows, *columns)


def largest_over(largest, *moves):
    for move in moves:
        largest = jnp.maximum(largest, send(largest, pairs(move)))
    return largest


def scales(largest, tokens_total):
    largest = jnp.maximum(largest, 1e-18)
    most = largest * largest * tokens_total
    return 32768.0 / most, most / (32768.0 * tokens_total)


def far(p):
    _, _, second, third = p["partial"]
    a = send((second * p["down"]).astype(HALF), Z_ALONG)
    return {**p, "a": a, "c": send((third * p["down"]).astype(HALF), Z_AGAINST)}


def along(p):
    b = p["partial"][1] * p["down"] + p["a"].astype(jnp.float32)
    return {**p, "a": None, "b": send(b.astype(HALF), Z_ALONG)}


def summed(p):
    b, c = p["b"].astype(jnp.float32), p["c"].astype(jnp.float32)
    return p["partial"][0] * p["down"] + b + c


def near(p):
    total = summed(p)
    value = jnp.where(p["stays"], total[1], total[0])
    return {"total": total, "stays": p["stays"], "n": send(value.astype(HALF), Y_PARTNER)}


def cross(p):
    value = p["total"][1] + p["n"].astype(jnp.float32)
    return {**p, "m": send(value.astype(HALF), Y_MIDDLE)}


def result(p):
    own = p["total"][0] + p["n"].astype(jnp.float32)
    return jnp.where(p["stays"], own, p["m"].astype(jnp.float32))


def direct(p):
    total = summed(p)
    value = jnp.where(p["stays"], total[1], total[0])
    n, m = send(value.astype(HALF), Y_ROUND), send(total[1].astype(HALF), Y_MIDDLE)
    return {"total": total[0], "stays": p["stays"], "n": n, "m": m}


def direct_result(p):
    other = jnp.where(p["stays"], p["total"], p["m"].astype(jnp.float32))
    return p["n"].astype(jnp.float32) + other


def turned_product(basis, queries):
    return lax.dot_general(
        basis, queries, (((0,), (1,)), ((), ())), preferred_element_type=jnp.float32
    )


def give(value, bit, to):
    rows = value.shape[0] // 2
    return (value, send(lax.dynamic_slice_in_dim(value, (1 - bit) * rows, rows, 0), to))


def add(value, got, bit):
    rows = got.shape[0]
    return lax.dynamic_slice_in_dim(value, bit * rows, rows, 0) + got


def join(value, to, bit, axis):
    got = send(value, to)
    return jnp.where(
        bit == 0,
        jnp.concatenate([value, got], axis=axis),
        jnp.concatenate([got, value], axis=axis),
    )


def round_x(rows):
    return lax.all_gather(rows, AXES, axis_index_groups=X_RINGS)


def on_device(activations, out_grads, act_basis, grad_basis, query_acts, query_grads):
    dp, block = lax.axis_index("dp"), lax.axis_index("block")
    x, y_hi, z, y_lo, core = block // 2, block % 2, dp // 4, dp // 2 % 2, dp % 2
    tokens_total = activations.shape[0] * lax.axis_size("dp")
    along_z = 1 - 2 * core
    slot = jnp.stack([((d - z) * along_z) % 4 for d in range(4)]).astype(jnp.int32)
    half = out_grads.shape[1] // 2

    mine, theirs = turn(activations, core)
    other = send(activations, OTHER_COLUMN)
    got = send(theirs, SIBLING)
    rows_1 = round_x(jnp.stack([mine[:FIRST], got[:FIRST]]))
    rows_2 = round_x(jnp.stack([mine[FIRST:], got[FIRST:]]))
    sibling = send(activations, SIBLING)
    grads = jnp.pad(out_grads.T, ((0, -out_grads.shape[1] % 16), (0, 0)))
    grad_mine = lax.dynamic_slice_in_dim(grads, core * half, half, 0)
    grad_theirs = lax.dynamic_slice_in_dim(grads, (1 - core) * half, half, 0)
    grad_rows = jnp.stack([grad_mine, send(grad_theirs, SIBLING)])
    grad_rows = round_x(jnp.pad(grad_rows, ((0, 0), (0, -half % 16), (0, 0))))
    grad_sibling = send(grads, SIBLING)
    part = jnp.concatenate(
        [turned_product(act_basis, query_acts), turned_product(grad_basis, query_grads)], axis=0
    )
    part = jnp.pad(part, ((0, -part.shape[0] % 64), (0, 0)))
    largest = largest_over(
        jnp.where(
            lax.broadcasted_iota(jnp.int32, (8, 128), 0) < 4,
            jnp.max(jnp.abs(activations)).astype(jnp.float32),
            jnp.max(jnp.abs(out_grads)).astype(jnp.float32),
        ),
        lambda x, y, z, c: (x, y, z, c + 1),
        lambda x, y, z, c: (x, y, z ^ 1, c),
        lambda x, y, z, c: (x, y, z + 2, c),
        lambda x, y, z, c: (x ^ 1, y, z, c),
        lambda x, y, z, c: (x + 2, y, z, c),
    )
    largest, other, sibling, grads, grad_sibling, part = lax.optimization_barrier(
        (largest, other, sibling, grads, grad_sibling, part)
    )
    largest = largest_over(
        largest, lambda x, y, z, c: (x, y ^ 1, z, c), lambda x, y, z, c: (x, y + 2, z, c)
    )
    act_down, act_up = scales(largest[0, 0], tokens_total)
    grad_down, grad_up = scales(largest[4, 0], tokens_total)
    columns = [activations, sibling, other, send(other, SIBLING)]
    columns, rows_1, grads, grad_sibling, part, act_down, act_up, grad_down, grad_up = (
        lax.optimization_barrier(
            (columns, rows_1, grads, grad_sibling, part, act_down, act_up, grad_down, grad_up)
        )
    )

    parts, done, beside = [None] * 3, [None] * 3, ()
    steps = [(far, along, near, cross)] * 2 + [(far, along, direct)]
    for stage in range(6):
        for i in reversed(range(len(parts))):
            step = stage - i - 1
            if 0 <= step < len(steps[i]):
                down = grad_down if i == 2 else act_down
                parts[i] = steps[i][step]({**parts[i], "down": down})
        if stage == 0:
            part = give(part, y_hi, OTHER_COLUMN)
            partial = products(slot, rows_1, columns)
            beside = send(grads, OTHER_COLUMN)
        elif stage == 1:
            part = give(add(*part, y_hi), x // 2, X_FAR)
            partial = products(slot, rows_2, columns)
            beside = [grads, grad_sibling, beside, send(beside, SIBLING)]
        elif stage == 2:
            part = give(add(*part, x // 2), x % 2, X_FLIP)
            partial = products(slot, grad_rows, beside, turned=True)
            beside = ()
        elif stage == 3:
            part = add(*part, x % 2)
            part = part.reshape((1, 1, 1, *part.shape))
            part = join(join(part, OTHER_COLUMN, y_hi, 0), X_FLIP, x % 2, 2)
        elif stage == 4:
            part = join(part, X_FAR, x // 2, 1)
        if stage < len(parts):
            parts[stage] = {"partial": partial, "stays": y_lo == y_hi}
        if stage < 5:
            parts, part, beside = lax.optimization_barrier((parts, part, beside))
    act_cov = jnp.concatenate([result(parts[0]), result(parts[1])], axis=0) * act_up
    grad_cov = direct_result(parts[2])[:half, : out_grads.shape[1]] * grad_up
    part = part.reshape(-1, query_acts.shape[0])
    split, end = act_basis.shape[1], act_basis.shape[1] + grad_basis.shape[1]
    return (act_cov, grad_cov, part[:split].T, part[split:end].T)


def solution(mesh):
    return jax.shard_map(
        on_device,
        mesh=mesh,
        in_specs=(
            P("dp", "block"),
            P("dp", "block"),
            P("block", "dp"),
            P("block", "dp"),
            P(None, "block"),
            P(None, "block"),
        ),
        out_specs=(P("dp", "block"), P("dp", "block"), P(None, "dp"), P(None, "dp")),
        check_vma=False,
    )
```

```python
import functools
import itertools

import jax
import jax.numpy as jnp
from jax import lax
from jax.experimental import pallas as pl
from jax.experimental.pallas import tpu as pltpu
from jax.sharding import PartitionSpec as P

AXES = ("dp", "block")
HALF = jnp.float16


def place(x, y, z, core):
    return ((z * 2 + y % 2) * 2 + core) * 8 + x * 2 + y // 2


def pairs(move):
    out = []
    for at in itertools.product(range(4), range(4), range(4), range(2)):
        x, y, z, core = move(*at)
        out.append((place(*at), place(x % 4, y % 4, z % 4, core % 2)))
    return out


SIBLING = pairs(lambda x, y, z, c: (x, y, z, c + 1))
OTHER_COLUMN = pairs(lambda x, y, z, c: (x, y + 2, z, c))
X_DOWN = pairs(lambda x, y, z, c: (x - 1, y, z, c))
X_UP = pairs(lambda x, y, z, c: (x + 1, y, z, c))
X_FAR = pairs(lambda x, y, z, c: (x + 2, y, z, c))
Z_ALONG = pairs(lambda x, y, z, c: (x, y, z + 1 - 2 * c, c))
Z_AGAINST = pairs(lambda x, y, z, c: (x, y, z - 1 + 2 * c, c))
X_RINGS = [
    [place(x, y, z, c) for x in range(4)]
    for y, z, c in itertools.product(range(4), range(4), range(2))
]
FIRST = 304
Y_PARTNER = pairs(lambda x, y, z, c: (x, y ^ 1, z, c))
Y_ROUND = pairs(lambda x, y, z, c: (x, (2, 0, 3, 1)[y], z, c))
Y_MIDDLE = [p for p in pairs(lambda x, y, z, c: (x, (0, 2, 1, 3)[y], z, c)) if p[0] != p[1]]


def send(value, to):
    return lax.ppermute(value, AXES, to)


def turn_kernel(core, own, mine, theirs, turned):
    half = mine.shape[0]
    turned[...] = own[...].T
    mine[...] = turned[pl.ds(pl.multiple_of(core[0] * half, 16), half), :]
    theirs[...] = turned[pl.ds(pl.multiple_of((1 - core[0]) * half, 16), half), :]


def turn(own, core):
    tokens, width = own.shape
    vmem = pl.BlockSpec(memory_space=pltpu.VMEM)
    half = jax.ShapeDtypeStruct((width // 2, tokens), own.dtype)
    return pl.pallas_call(
        turn_kernel,
        out_shape=(half, half),
        in_specs=[pl.BlockSpec(memory_space=pltpu.SMEM), vmem],
        out_specs=(vmem, vmem),
        scratch_shapes=[pltpu.VMEM((width, tokens), own.dtype)],
        compiler_params=pltpu.CompilerParams(vmem_limit_bytes=24 << 20),
    )(core.reshape(1).astype(jnp.int32), own)


def product_kernel(kinds, slots, source, rows, *refs):
    count = len(slots)
    columns_of, refs = refs[: 4 * len(kinds)], refs[4 * len(kinds) :]
    outs, refs = refs[:count], refs[count:]
    *buffers, sem = refs
    block, at = pl.program_id(0), pl.program_id(1)
    start, column_waits, row_waits, work = [], ([], []), [[] for _ in slots], []
    lane = 0
    for kind, (first, turned) in enumerate(kinds):
        held, columns, landing = buffers[3 * kind : 3 * kind + 3]
        n, tokens = held.shape[1], held.shape[2] // 2
        width = columns.shape[2]
        part = [pl.ds(half * tokens, tokens) for half in (0, 1)]
        for i in (0, 1):
            for half in (0, 1):
                ref = columns_of[4 * kind + 2 * i + half]
                if turned:
                    place = landing.at[i, :, part[half]]
                else:
                    place = columns.at[i, part[half], :]
                column_waits[i].append(
                    pltpu.make_async_copy(ref, place, sem.at[kind, half, i])
                )
        for i, slot in enumerate(slots):
            for half in (0, 1):
                row_waits[i].append(
                    pltpu.make_async_copy(
                        rows.at[source[slot], half, pl.ds(first, n), :],
                        held.at[i, :, part[half]],
                        sem.at[kind, half, 2 + i],
                    )
                )
        work.append((held, columns, landing if turned else None, lane, width))
        lane += width

    @pl.when((block == 0) & (at == 0))
    def _():
        for copy in column_waits[0] + sum(row_waits, []) + column_waits[1]:
            copy.start()

    for i in (0, 1):

        @pl.when((block == i) & (at == 0))
        def _(i=i):
            for copy in column_waits[i]:
                copy.wait()
            for _, columns, landing, _, _ in work:
                if landing is not None:
                    columns[i] = landing[i].T

    for i in range(count):

        @pl.when((block == 0) & (at == i))
        def _(i=i):
            for copy in row_waits[i]:
                copy.wait()

    for i, out in enumerate(outs):

        @pl.when(at == i)
        def _(i=i, out=out):
            for held, columns, _, lane, width in work:
                out[0, :, lane : lane + width] = jnp.dot(
                    held[i], columns[block], preferred_element_type=jnp.float32
                )


def products(source, slots, rows, n, columns, grad_columns=()):
    tokens = rows.shape[3]
    dtype = rows.dtype
    count = len(slots)
    kinds, widths, buffers = [(0, False)], [columns[0].shape[1]], []
    if grad_columns:
        kinds.append((n, True))
        widths.append(grad_columns[0].shape[0])
    for (_, turned), width in zip(kinds, widths):
        buffers += [
            pltpu.VMEM((count, n, 2 * tokens), dtype),
            pltpu.VMEM((2, 2 * tokens, width), dtype),
            pltpu.VMEM((2, width, 2 * tokens) if turned else (16, 128), dtype),
        ]
    anywhere = pl.BlockSpec(memory_space=pl.ANY)
    smem = pl.BlockSpec(memory_space=pltpu.SMEM)
    return pl.pallas_call(
        functools.partial(product_kernel, kinds, slots),
        out_shape=[jax.ShapeDtypeStruct((2, n, sum(widths)), jnp.float32)] * count,
        grid=(2, count),
        in_specs=[smem] + [anywhere] * (1 + 4 * len(kinds)),
        out_specs=[pl.BlockSpec((1, n, sum(widths)), lambda block, at: (block, 0, 0))] * count,
        scratch_shapes=[*buffers, pltpu.SemaphoreType.DMA((len(kinds), 2, 2 + count))],
        compiler_params=pltpu.CompilerParams(vmem_limit_bytes=60 << 20),
        cost_estimate=pl.CostEstimate(
            flops=4 * count * n * tokens * sum(widths),
            bytes_accessed=4 * count * n * tokens,
            transcendentals=0,
        ),
    )(source, rows, *columns, *grad_columns)


def largest_over(largest, *moves):
    for move in moves:
        largest = jnp.maximum(largest, send(largest, pairs(move)))
    return largest


def scales(largest, tokens_total):
    largest = jnp.maximum(largest, 1e-18)
    most = largest * largest * tokens_total
    return 32768.0 / most, most / (32768.0 * tokens_total)


def far(p):
    second, third = p.pop("far")
    a = send((second * p["down"]).astype(HALF), Z_ALONG)
    return {**p, "a": a, "c": send((third * p["down"]).astype(HALF), Z_AGAINST)}


def along(p):
    b = p["close"][1] * p["down"] + p["a"].astype(jnp.float32)
    return {**p, "a": None, "b": send(b.astype(HALF), Z_ALONG)}


def summed(p):
    b, c = p["b"].astype(jnp.float32), p["c"].astype(jnp.float32)
    return p["close"][0] * p["down"] + b + c


def near(p, stays):
    total = summed(p)
    value = jnp.where(stays, total[1], total[0])
    return {"total": total, "n": send(value.astype(HALF), Y_PARTNER)}


def cross(p):
    value = p["total"][1] + p["n"].astype(jnp.float32)
    return {**p, "m": send(value.astype(HALF), Y_MIDDLE)}


def crossed(p, stays):
    own = p["total"][0] + p["n"].astype(jnp.float32)
    return jnp.where(stays, own, p["m"].astype(jnp.float32))


def across(p, stays):
    total = summed(p)
    value = jnp.where(stays, total[1], total[0])
    n, m = send(value.astype(HALF), Y_ROUND), send(total[1].astype(HALF), Y_MIDDLE)
    return {"total": total, "n": n, "m": m}


def result(p, stays):
    other = jnp.where(stays, p["total"][0], p["m"].astype(jnp.float32))
    return p["n"].astype(jnp.float32) + other


def turned_product(basis, queries):
    return lax.dot_general(
        basis, queries, (((0,), (1,)), ((), ())), preferred_element_type=jnp.float32
    )


def give(value, bit, to, axis):
    return (value, send(lax.dynamic_slice_in_dim(value, 1 - bit, 1, axis), to))


def add(value, got, bit, axis):
    return lax.dynamic_slice_in_dim(value, bit, 1, axis) + got


def scatter_x(value, x):
    quarter = [
        lax.dynamic_index_in_dim(value[:, 0], (x + d) % 4, 0, keepdims=False) for d in range(4)
    ]
    return [quarter[0]] + [send(q, to) for q, to in zip(quarter[1:], (X_UP, X_FAR, X_DOWN))]


def round_x(rows):
    return lax.all_gather(rows, AXES, axis_index_groups=X_RINGS)


def on_device(activations, out_grads, act_basis, grad_basis, query_acts, query_grads):
    dp, block = lax.axis_index("dp"), lax.axis_index("block")
    x, y_hi, z, y_lo, core = block // 2, block % 2, dp // 4, dp // 2 % 2, dp % 2
    tokens_total = activations.shape[0] * lax.axis_size("dp")
    source = jnp.stack([(z + d * (1 - 2 * core)) % 4 for d in range(4)]).astype(jnp.int32)
    half = out_grads.shape[1] // 2

    mine, theirs = turn(activations, core)
    other = send(activations, OTHER_COLUMN)
    got = send(theirs, SIBLING)
    rows_1 = round_x(jnp.stack([mine[:FIRST], got[:FIRST]]))
    rows_2 = jnp.stack([mine[FIRST:], got[FIRST:]])
    sibling = send(activations, SIBLING)
    grads = jnp.pad(out_grads.T, ((0, -out_grads.shape[1] % 16), (0, 0)))
    grad_mine = lax.dynamic_slice_in_dim(grads, core * half, half, 0)
    grad_theirs = lax.dynamic_slice_in_dim(grads, (1 - core) * half, half, 0)
    grad_rows = jnp.stack([grad_mine, send(grad_theirs, SIBLING)])
    grad_rows = jnp.pad(grad_rows, ((0, 0), (0, rows_2.shape[1] - half), (0, 0)))
    grad_sibling = send(grads, SIBLING)
    part = jnp.concatenate(
        [turned_product(act_basis, query_acts), turned_product(grad_basis, query_grads)], axis=0
    )
    queries = query_acts.shape[0]
    part = jnp.pad(part, ((0, -part.shape[0] % 64), (0, 0))).reshape(4, 2, -1, queries)
    largest = largest_over(
        jnp.where(
            lax.broadcasted_iota(jnp.int32, (8, 128), 0) < 4,
            jnp.max(jnp.abs(activations)).astype(jnp.float32),
            jnp.max(jnp.abs(out_grads)).astype(jnp.float32),
        ),
        lambda x, y, z, c: (x, y, z, c + 1),
        lambda x, y, z, c: (x, y, z ^ 1, c),
        lambda x, y, z, c: (x, y, z + 2, c),
        lambda x, y, z, c: (x ^ 1, y, z, c),
        lambda x, y, z, c: (x + 2, y, z, c),
    )
    n_2 = rows_2.shape[1]
    rows_2 = jnp.concatenate([rows_2, grad_rows], axis=1)
    largest, other, sibling, grads, rows_2, grad_sibling, part = lax.optimization_barrier(
        (largest, other, sibling, grads, rows_2, grad_sibling, part)
    )
    rows_2 = round_x(rows_2)
    largest = largest_over(
        largest, lambda x, y, z, c: (x, y ^ 1, z, c), lambda x, y, z, c: (x, y + 2, z, c)
    )
    act_down, act_up = scales(largest[0, 0], tokens_total)
    grad_down, grad_up = scales(largest[4, 0], tokens_total)
    columns = [activations, sibling, other, send(other, SIBLING)]
    columns, rows_1, grads, grad_sibling, part, act_down, act_up, grad_down, grad_up = (
        lax.optimization_barrier(
            (columns, rows_1, grads, grad_sibling, part, act_down, act_up, grad_down, grad_up)
        )
    )

    width, grad_width = activations.shape[1], grads.shape[0]
    down = jnp.where(jnp.arange(width + grad_width) < width, act_down, grad_down)
    one, two = {"down": act_down}, {"down": down}
    stays = y_lo == y_hi
    one["far"] = products(source, (2, 3), rows_1, FIRST, columns)
    grad_other = send(grads, OTHER_COLUMN)
    one, grad_other = lax.optimization_barrier((one, grad_other))

    one = far(one)
    part = give(part, y_hi, OTHER_COLUMN, 1)
    one["close"] = products(source, (0, 1), rows_1, FIRST, columns)
    grad_columns = [grads, grad_sibling, grad_other, send(grad_other, SIBLING)]
    one, part, grad_columns = lax.optimization_barrier((one, part, grad_columns))

    one = along(one)
    part = scatter_x(add(*part, y_hi, 1), x)
    two["far"] = products(source, (2, 3), rows_2, n_2, columns, grad_columns)
    one, two, part = lax.optimization_barrier((one, two, part))

    part = sum(part)
    part = (part, send(part, OTHER_COLUMN))
    one, two = near(one, stays), far(two)
    two["close"] = products(source, (0, 1), rows_2, n_2, columns, grad_columns)
    one, two, part = lax.optimization_barrier((one, two, part))

    part = round_x(jnp.where(y_hi == 0, jnp.stack(part), jnp.stack(part[::-1])))
    one = cross(one)
    two = along(two)
    one, two = lax.optimization_barrier((one, two))

    two = across(two, stays)
    act_cov = jnp.concatenate(
        [crossed(one, stays), result(two, stays)[:, :width]], axis=0
    )
    grad_cov = result(two, stays)[:half, width : width + out_grads.shape[1]]
    part = part.reshape(-1, queries)
    split, end = act_basis.shape[1], act_basis.shape[1] + grad_basis.shape[1]
    return (act_cov * act_up, grad_cov * grad_up, part[:split].T, part[split:end].T)


def solution(mesh):
    return jax.shard_map(
        on_device,
        mesh=mesh,
        in_specs=(
            P("dp", "block"),
            P("dp", "block"),
            P("block", "dp"),
            P("block", "dp"),
            P(None, "block"),
            P(None, "block"),
        ),
        out_specs=(P("dp", "block"), P("dp", "block"), P(None, "dp"), P(None, "dp")),
        check_vma=False,
    )
```

```python
import functools
import itertools

import jax
import jax.numpy as jnp
from jax import lax
from jax.experimental import pallas as pl
from jax.experimental.pallas import tpu as pltpu
from jax.sharding import PartitionSpec as P

AXES = ("dp", "block")
HALF = jnp.float16


def place(x, y, z, core):
    return ((z * 2 + y % 2) * 2 + core) * 8 + x * 2 + y // 2


def pairs(move):
    out = []
    for at in itertools.product(range(4), range(4), range(4), range(2)):
        x, y, z, core = move(*at)
        out.append((place(*at), place(x % 4, y % 4, z % 4, core % 2)))
    return out


SIBLING = pairs(lambda x, y, z, c: (x, y, z, c + 1))
OTHER_COLUMN = pairs(lambda x, y, z, c: (x, y + 2, z, c))
X_DOWN = pairs(lambda x, y, z, c: (x - 1, y, z, c))
X_UP = pairs(lambda x, y, z, c: (x + 1, y, z, c))
X_FAR = pairs(lambda x, y, z, c: (x + 2, y, z, c))
Z_ALONG = pairs(lambda x, y, z, c: (x, y, z + 1 - 2 * c, c))
Z_AGAINST = pairs(lambda x, y, z, c: (x, y, z - 1 + 2 * c, c))
X_RINGS = [
    [place(x, y, z, c) for x in range(4)]
    for y, z, c in itertools.product(range(4), range(4), range(2))
]
FIRST = 304
Y_PARTNER = pairs(lambda x, y, z, c: (x, y ^ 1, z, c))
Y_ROUND = pairs(lambda x, y, z, c: (x, (2, 0, 3, 1)[y], z, c))
Y_MIDDLE = [p for p in pairs(lambda x, y, z, c: (x, (0, 2, 1, 3)[y], z, c)) if p[0] != p[1]]


def send(value, to):
    return lax.ppermute(value, AXES, to)


def turn_kernel(core, own, mine, theirs, turned):
    half = mine.shape[0]
    turned[...] = own[...].T
    mine[...] = turned[pl.ds(pl.multiple_of(core[0] * half, 16), half), :]
    theirs[...] = turned[pl.ds(pl.multiple_of((1 - core[0]) * half, 16), half), :]


def turn(own, core):
    tokens, width = own.shape
    vmem = pl.BlockSpec(memory_space=pltpu.VMEM)
    half = jax.ShapeDtypeStruct((width // 2, tokens), own.dtype)
    return pl.pallas_call(
        turn_kernel,
        out_shape=(half, half),
        in_specs=[pl.BlockSpec(memory_space=pltpu.SMEM), vmem],
        out_specs=(vmem, vmem),
        scratch_shapes=[pltpu.VMEM((width, tokens), own.dtype)],
        compiler_params=pltpu.CompilerParams(vmem_limit_bytes=24 << 20),
    )(core.reshape(1).astype(jnp.int32), own)


def product_kernel(kinds, slots, source, rows, *refs):
    count = len(slots)
    columns_of, refs = refs[: 4 * len(kinds)], refs[4 * len(kinds) :]
    outs, refs = refs[:count], refs[count:]
    *buffers, sem = refs
    block, at = pl.program_id(0), pl.program_id(1)
    start, column_waits, row_waits, work = [], ([], []), [[] for _ in slots], []
    lane = 0
    for kind, (first, turned) in enumerate(kinds):
        held, columns, landing = buffers[3 * kind : 3 * kind + 3]
        n, tokens = held.shape[1], held.shape[2] // 2
        width = columns.shape[2]
        part = [pl.ds(half * tokens, tokens) for half in (0, 1)]
        for i in (0, 1):
            for half in (0, 1):
                ref = columns_of[4 * kind + 2 * i + half]
                if turned:
                    place = landing.at[i, :, part[half]]
                else:
                    place = columns.at[i, part[half], :]
                column_waits[i].append(
                    pltpu.make_async_copy(ref, place, sem.at[kind, half, i])
                )
        for i, slot in enumerate(slots):
            for half in (0, 1):
                row_waits[i].append(
                    pltpu.make_async_copy(
                        rows.at[source[slot], half, pl.ds(first, n), :],
                        held.at[i, :, part[half]],
                        sem.at[kind, half, 2 + i],
                    )
                )
        work.append((held, columns, landing if turned else None, lane, width))
        lane += width

    @pl.when((block == 0) & (at == 0))
    def _():
        for copy in column_waits[0] + sum(row_waits, []) + column_waits[1]:
            copy.start()

    for i in (0, 1):

        @pl.when((block == i) & (at == 0))
        def _(i=i):
            for copy in column_waits[i]:
                copy.wait()
            for _, columns, landing, _, _ in work:
                if landing is not None:
                    columns[i] = landing[i].T

    for i in range(count):

        @pl.when((block == 0) & (at == i))
        def _(i=i):
            for copy in row_waits[i]:
                copy.wait()

    for i, out in enumerate(outs):

        @pl.when(at == i)
        def _(i=i, out=out):
            for held, columns, _, lane, width in work:
                out[0, :, lane : lane + width] = jnp.dot(
                    held[i], columns[block], preferred_element_type=jnp.float32
                )


def products(source, slots, rows, n, columns, grad_columns=()):
    tokens = rows.shape[3]
    dtype = rows.dtype
    count = len(slots)
    kinds, widths, buffers = [(0, False)], [columns[0].shape[1]], []
    if grad_columns:
        kinds.append((n, True))
        widths.append(grad_columns[0].shape[0])
    for (_, turned), width in zip(kinds, widths):
        buffers += [
            pltpu.VMEM((count, n, 2 * tokens), dtype),
            pltpu.VMEM((2, 2 * tokens, width), dtype),
            pltpu.VMEM((2, width, 2 * tokens) if turned else (16, 128), dtype),
        ]
    anywhere = pl.BlockSpec(memory_space=pl.ANY)
    smem = pl.BlockSpec(memory_space=pltpu.SMEM)
    return pl.pallas_call(
        functools.partial(product_kernel, kinds, slots),
        out_shape=[jax.ShapeDtypeStruct((2, n, sum(widths)), jnp.float32)] * count,
        grid=(2, count),
        in_specs=[smem] + [anywhere] * (1 + 4 * len(kinds)),
        out_specs=[pl.BlockSpec((1, n, sum(widths)), lambda block, at: (block, 0, 0))] * count,
        scratch_shapes=[*buffers, pltpu.SemaphoreType.DMA((len(kinds), 2, 2 + count))],
        compiler_params=pltpu.CompilerParams(vmem_limit_bytes=60 << 20),
        cost_estimate=pl.CostEstimate(
            flops=4 * count * n * tokens * sum(widths),
            bytes_accessed=4 * count * n * tokens,
            transcendentals=0,
        ),
    )(source, rows, *columns, *grad_columns)


def largest_over(largest, *moves):
    for move in moves:
        largest = jnp.maximum(largest, send(largest, pairs(move)))
    return largest


def scales(largest, tokens_total):
    largest = jnp.maximum(largest, 1e-18)
    most = largest * largest * tokens_total
    return 32768.0 / most, most / (32768.0 * tokens_total)


def along(p):
    b = p["close"][1] * p["down"] + p["a"].astype(jnp.float32)
    return {**p, "a": None, "b": send(b.astype(HALF), Z_ALONG)}


def summed(p):
    b, c = p["b"].astype(jnp.float32), p["c"].astype(jnp.float32)
    return p["close"][0] * p["down"] + b + c


def crossing(p):
    return (p["total"][1] + p["n"].astype(jnp.float32)).astype(HALF)


def crossed(p, stays):
    own = p["total"][0] + p["n"].astype(jnp.float32)
    return jnp.where(stays, own, p["m"].astype(jnp.float32))


def across(p, stays):
    total = summed(p)
    value = jnp.where(stays, total[1], total[0])
    n, m = send(value.astype(HALF), Y_ROUND), send(total[1].astype(HALF), Y_MIDDLE)
    return {"total": total, "n": n, "m": m}


def result(p, stays):
    other = jnp.where(stays, p["total"][0], p["m"].astype(jnp.float32))
    return p["n"].astype(jnp.float32) + other


def turned_product(basis, queries):
    return lax.dot_general(
        basis, queries, (((0,), (1,)), ((), ())), preferred_element_type=jnp.float32
    )


def give(value, bit, to, axis):
    return (value, send(lax.dynamic_slice_in_dim(value, 1 - bit, 1, axis), to))


def add(value, got, bit, axis):
    return lax.dynamic_slice_in_dim(value, bit, 1, axis) + got


def scatter_x(value, x):
    quarter = [
        lax.dynamic_index_in_dim(value[:, 0], (x + d) % 4, 0, keepdims=False) for d in range(4)
    ]
    return [quarter[0]] + [send(q, to) for q, to in zip(quarter[1:], (X_UP, X_FAR, X_DOWN))]


def round_x(rows):
    return lax.all_gather(rows, AXES, axis_index_groups=X_RINGS)


def on_device(activations, out_grads, act_basis, grad_basis, query_acts, query_grads):
    dp, block = lax.axis_index("dp"), lax.axis_index("block")
    x, y_hi, z, y_lo, core = block // 2, block % 2, dp // 4, dp // 2 % 2, dp % 2
    tokens_total = activations.shape[0] * lax.axis_size("dp")
    source = jnp.stack([(z + d * (1 - 2 * core)) % 4 for d in range(4)]).astype(jnp.int32)
    half = out_grads.shape[1] // 2

    mine, theirs = turn(activations, core)
    other = send(activations, OTHER_COLUMN)
    got = send(theirs, SIBLING)
    rows_1 = round_x(jnp.stack([mine[:FIRST], got[:FIRST]]))
    rows_2 = jnp.stack([mine[FIRST:], got[FIRST:]])
    sibling = send(activations, SIBLING)
    grads = jnp.pad(out_grads.T, ((0, -out_grads.shape[1] % 16), (0, 0)))
    grad_mine = lax.dynamic_slice_in_dim(grads, core * half, half, 0)
    grad_theirs = lax.dynamic_slice_in_dim(grads, (1 - core) * half, half, 0)
    grad_rows = jnp.stack([grad_mine, send(grad_theirs, SIBLING)])
    grad_rows = jnp.pad(grad_rows, ((0, 0), (0, rows_2.shape[1] - half), (0, 0)))
    grad_sibling = send(grads, SIBLING)
    part = jnp.concatenate(
        [turned_product(act_basis, query_acts), turned_product(grad_basis, query_grads)], axis=0
    )
    queries = query_acts.shape[0]
    part = jnp.pad(part, ((0, -part.shape[0] % 64), (0, 0))).reshape(4, 2, -1, queries)
    largest = largest_over(
        jnp.where(
            lax.broadcasted_iota(jnp.int32, (8, 128), 0) < 4,
            jnp.max(jnp.abs(activations)).astype(jnp.float32),
            jnp.max(jnp.abs(out_grads)).astype(jnp.float32),
        ),
        lambda x, y, z, c: (x, y, z, c + 1),
        lambda x, y, z, c: (x, y, z ^ 1, c),
        lambda x, y, z, c: (x, y, z + 2, c),
        lambda x, y, z, c: (x ^ 1, y, z, c),
        lambda x, y, z, c: (x + 2, y, z, c),
    )
    n_2 = rows_2.shape[1]
    rows_2 = jnp.concatenate([rows_2, grad_rows], axis=1)
    largest, other, sibling, grads, rows_2, grad_sibling, part = lax.optimization_barrier(
        (largest, other, sibling, grads, rows_2, grad_sibling, part)
    )
    rows_2 = round_x(rows_2)
    largest = largest_over(
        largest, lambda x, y, z, c: (x, y ^ 1, z, c), lambda x, y, z, c: (x, y + 2, z, c)
    )
    act_down, act_up = scales(largest[0, 0], tokens_total)
    grad_down, grad_up = scales(largest[4, 0], tokens_total)
    columns = [activations, sibling, other, send(other, SIBLING)]
    columns, rows_1, grads, grad_sibling, part, act_down, act_up, grad_down, grad_up = (
        lax.optimization_barrier(
            (columns, rows_1, grads, grad_sibling, part, act_down, act_up, grad_down, grad_up)
        )
    )

    width, grad_width = activations.shape[1], grads.shape[0]
    down = jnp.where(jnp.arange(width + grad_width) < width, act_down, grad_down)
    stays = y_lo == y_hi
    second, third = products(source, (2, 3), rows_1, FIRST, columns)
    grad_other = send(grads, OTHER_COLUMN)
    a = send((second * act_down).astype(HALF), Z_ALONG)
    c = send((third * act_down).astype(HALF), Z_AGAINST)
    close = products(source, (0, 1), rows_1, FIRST, columns)
    part = give(part, y_hi, OTHER_COLUMN, 1)
    grad_columns = [grads, grad_sibling, grad_other, send(grad_other, SIBLING)]
    message = (close[1] * act_down + a.astype(jnp.float32)).astype(HALF)
    message, rows_2, part = lax.optimization_barrier((message, rows_2, part))
    one = {"close": close, "down": act_down, "b": send(message, Z_ALONG), "c": c}

    second, third = products(source, (2, 3), rows_2, n_2, columns, grad_columns)
    part = scatter_x(add(*part, y_hi, 1), x)
    total = summed(one)
    messages = (
        (second * down).astype(HALF),
        (third * down).astype(HALF),
        jnp.where(stays, total[1], total[0]).astype(HALF),
    )
    messages, rows_2 = lax.optimization_barrier((messages, rows_2))
    a, c = send(messages[0], Z_ALONG), send(messages[1], Z_AGAINST)
    one = {"total": total, "n": send(messages[2], Y_PARTNER)}
    two = {"close": products(source, (0, 1), rows_2, n_2, columns, grad_columns)}
    two = {**two, "down": down, "a": a, "c": c}
    part = sum(part)
    part = (part, send(part, OTHER_COLUMN))

    message = crossing(one)
    message, two = lax.optimization_barrier((message, two))
    one["m"] = send(message, Y_MIDDLE)
    two = along(two)
    part = round_x(jnp.where(y_hi == 0, jnp.stack(part), jnp.stack(part[::-1])))

    two = across(two, stays)
    act_cov = jnp.concatenate(
        [crossed(one, stays), result(two, stays)[:, :width]], axis=0
    )
    grad_cov = result(two, stays)[:half, width : width + out_grads.shape[1]]
    part = part.reshape(-1, queries)
    split, end = act_basis.shape[1], act_basis.shape[1] + grad_basis.shape[1]
    return (act_cov * act_up, grad_cov * grad_up, part[:split].T, part[split:end].T)


def solution(mesh):
    return jax.shard_map(
        on_device,
        mesh=mesh,
        in_specs=(
            P("dp", "block"),
            P("dp", "block"),
            P("block", "dp"),
            P("block", "dp"),
            P(None, "block"),
            P(None, "block"),
        ),
        out_specs=(P("dp", "block"), P("dp", "block"), P(None, "dp"), P(None, "dp")),
        check_vma=False,
    )
```

```python
import functools
import itertools

import jax
import jax.numpy as jnp
from jax import lax
from jax.experimental import pallas as pl
from jax.experimental.pallas import tpu as pltpu
from jax.sharding import PartitionSpec as P

AXES = ("dp", "block")
HALF = jnp.float16


def place(x, y, z, core):
    return ((z * 2 + y % 2) * 2 + core) * 8 + x * 2 + y // 2


def pairs(move):
    out = []
    for at in itertools.product(range(4), range(4), range(4), range(2)):
        x, y, z, core = move(*at)
        out.append((place(*at), place(x % 4, y % 4, z % 4, core % 2)))
    return out


SIBLING = pairs(lambda x, y, z, c: (x, y, z, c + 1))
OTHER_COLUMN = pairs(lambda x, y, z, c: (x, y + 2, z, c))
X_DOWN = pairs(lambda x, y, z, c: (x - 1, y, z, c))
X_UP = pairs(lambda x, y, z, c: (x + 1, y, z, c))
X_FAR = pairs(lambda x, y, z, c: (x + 2, y, z, c))
Z_ALONG = pairs(lambda x, y, z, c: (x, y, z + 1 - 2 * c, c))
Z_AGAINST = pairs(lambda x, y, z, c: (x, y, z - 1 + 2 * c, c))
X_RINGS = [
    [place(x, y, z, c) for x in range(4)]
    for y, z, c in itertools.product(range(4), range(4), range(2))
]
FIRST = 304
Y_PARTNER = pairs(lambda x, y, z, c: (x, y ^ 1, z, c))
Y_ROUND = pairs(lambda x, y, z, c: (x, (2, 0, 3, 1)[y], z, c))
Y_MIDDLE = [p for p in pairs(lambda x, y, z, c: (x, (0, 2, 1, 3)[y], z, c)) if p[0] != p[1]]


def send(value, to):
    return lax.ppermute(value, AXES, to)


def turn_kernel(core, own, mine, theirs, turned):
    half = mine.shape[0]
    turned[...] = own[...].T
    mine[...] = turned[pl.ds(pl.multiple_of(core[0] * half, 16), half), :]
    theirs[...] = turned[pl.ds(pl.multiple_of((1 - core[0]) * half, 16), half), :]


def turn(own, core):
    tokens, width = own.shape
    vmem = pl.BlockSpec(memory_space=pltpu.VMEM)
    half = jax.ShapeDtypeStruct((width // 2, tokens), own.dtype)
    return pl.pallas_call(
        turn_kernel,
        out_shape=(half, half),
        in_specs=[pl.BlockSpec(memory_space=pltpu.SMEM), vmem],
        out_specs=(vmem, vmem),
        scratch_shapes=[pltpu.VMEM((width, tokens), own.dtype)],
        compiler_params=pltpu.CompilerParams(vmem_limit_bytes=24 << 20),
    )(core.reshape(1).astype(jnp.int32), own)


def product_kernel(kinds, slots, source, rows, *refs):
    count = len(slots)
    columns_of, refs = refs[: 4 * len(kinds)], refs[4 * len(kinds) :]
    outs, refs = refs[:count], refs[count:]
    *buffers, sem = refs
    block, at = pl.program_id(0), pl.program_id(1)
    start, column_waits, row_waits, work = [], ([], []), [[] for _ in slots], []
    lane = 0
    for kind, (first, turned) in enumerate(kinds):
        held, columns, landing = buffers[3 * kind : 3 * kind + 3]
        n, tokens = held.shape[1], held.shape[2] // 2
        width = columns.shape[2]
        part = [pl.ds(half * tokens, tokens) for half in (0, 1)]
        for i in (0, 1):
            for half in (0, 1):
                ref = columns_of[4 * kind + 2 * i + half]
                if turned:
                    place = landing.at[i, :, part[half]]
                else:
                    place = columns.at[i, part[half], :]
                column_waits[i].append(
                    pltpu.make_async_copy(ref, place, sem.at[kind, half, i])
                )
        for i, slot in enumerate(slots):
            for half in (0, 1):
                row_waits[i].append(
                    pltpu.make_async_copy(
                        rows.at[source[slot], half, pl.ds(first, n), :],
                        held.at[i, :, part[half]],
                        sem.at[kind, half, 2 + i],
                    )
                )
        work.append((held, columns, landing if turned else None, lane, width))
        lane += width

    @pl.when((block == 0) & (at == 0))
    def _():
        for copy in column_waits[0] + sum(row_waits, []) + column_waits[1]:
            copy.start()

    for i in (0, 1):

        @pl.when((block == i) & (at == 0))
        def _(i=i):
            for copy in column_waits[i]:
                copy.wait()
            for _, columns, landing, _, _ in work:
                if landing is not None:
                    columns[i] = landing[i].T

    for i in range(count):

        @pl.when((block == 0) & (at == i))
        def _(i=i):
            for copy in row_waits[i]:
                copy.wait()

    for i, out in enumerate(outs):

        @pl.when(at == i)
        def _(i=i, out=out):
            for held, columns, _, lane, width in work:
                out[0, :, lane : lane + width] = jnp.dot(
                    held[i], columns[block], preferred_element_type=jnp.float32
                )


def products(source, slots, rows, n, columns, grad_columns=()):
    tokens = rows.shape[3]
    dtype = rows.dtype
    count = len(slots)
    kinds, widths, buffers = [(0, False)], [columns[0].shape[1]], []
    if grad_columns:
        kinds.append((n, True))
        widths.append(grad_columns[0].shape[0])
    for (_, turned), width in zip(kinds, widths):
        buffers += [
            pltpu.VMEM((count, n, 2 * tokens), dtype),
            pltpu.VMEM((2, 2 * tokens, width), dtype),
            pltpu.VMEM((2, width, 2 * tokens) if turned else (16, 128), dtype),
        ]
    anywhere = pl.BlockSpec(memory_space=pl.ANY)
    smem = pl.BlockSpec(memory_space=pltpu.SMEM)
    return pl.pallas_call(
        functools.partial(product_kernel, kinds, slots),
        out_shape=[jax.ShapeDtypeStruct((2, n, sum(widths)), jnp.float32)] * count,
        grid=(2, count),
        in_specs=[smem] + [anywhere] * (1 + 4 * len(kinds)),
        out_specs=[pl.BlockSpec((1, n, sum(widths)), lambda block, at: (block, 0, 0))] * count,
        scratch_shapes=[*buffers, pltpu.SemaphoreType.DMA((len(kinds), 2, 2 + count))],
        compiler_params=pltpu.CompilerParams(vmem_limit_bytes=60 << 20),
        cost_estimate=pl.CostEstimate(
            flops=4 * count * n * tokens * sum(widths),
            bytes_accessed=4 * count * n * tokens,
            transcendentals=0,
        ),
    )(source, rows, *columns, *grad_columns)


def largest_over(largest, *moves):
    for move in moves:
        largest = jnp.maximum(largest, send(largest, pairs(move)))
    return largest


def scales(largest, tokens_total):
    largest = jnp.maximum(largest, 1e-18)
    most = largest * largest * tokens_total
    return 32768.0 / most, most


def mean(scaled, most, tokens_total):
    return scaled * (1.0 / (32768.0 * tokens_total)) * most


def along(p):
    b = p["close"][1] * p["down"] + p["a"].astype(jnp.float32)
    return {**p, "a": None, "b": send(b.astype(HALF), Z_ALONG)}


def summed(p):
    b, c = p["b"].astype(jnp.float32), p["c"].astype(jnp.float32)
    return p["close"][0] * p["down"] + b + c


def crossing(p):
    return (p["total"][1] + p["n"].astype(jnp.float32)).astype(HALF)


def crossed(p, stays):
    own = p["total"][0] + p["n"].astype(jnp.float32)
    return jnp.where(stays, own, p["m"].astype(jnp.float32))


def across(p, stays):
    total = summed(p)
    value = jnp.where(stays, total[1], total[0])
    n, m = send(value.astype(HALF), Y_ROUND), send(total[1].astype(HALF), Y_MIDDLE)
    return {"total": total, "n": n, "m": m}


def result(p, stays):
    other = jnp.where(stays, p["total"][0], p["m"].astype(jnp.float32))
    return p["n"].astype(jnp.float32) + other


def turned_product(basis, queries):
    return lax.dot_general(
        basis, queries, (((0,), (1,)), ((), ())), preferred_element_type=jnp.float32
    )


def give(value, bit, to, axis):
    return (value, send(lax.dynamic_slice_in_dim(value, 1 - bit, 1, axis), to))


def add(value, got, bit, axis):
    return lax.dynamic_slice_in_dim(value, bit, 1, axis) + got


def scatter_x(value, x):
    quarter = [
        lax.dynamic_index_in_dim(value[:, 0], (x + d) % 4, 0, keepdims=False) for d in range(4)
    ]
    return [quarter[0]] + [send(q, to) for q, to in zip(quarter[1:], (X_UP, X_FAR, X_DOWN))]


def round_x(rows):
    return lax.all_gather(rows, AXES, axis_index_groups=X_RINGS)


def on_device(activations, out_grads, act_basis, grad_basis, query_acts, query_grads):
    dp, block = lax.axis_index("dp"), lax.axis_index("block")
    x, y_hi, z, y_lo, core = block // 2, block % 2, dp // 4, dp // 2 % 2, dp % 2
    tokens_total = activations.shape[0] * lax.axis_size("dp")
    source = jnp.stack([(z + d * (1 - 2 * core)) % 4 for d in range(4)]).astype(jnp.int32)
    half = out_grads.shape[1] // 2

    mine, theirs = turn(activations, core)
    other = send(activations, OTHER_COLUMN)
    got = send(theirs, SIBLING)
    rows_1 = round_x(jnp.stack([mine[:FIRST], got[:FIRST]]))
    rows_2 = jnp.stack([mine[FIRST:], got[FIRST:]])
    sibling = send(activations, SIBLING)
    grads = jnp.pad(out_grads.T, ((0, -out_grads.shape[1] % 16), (0, 0)))
    grad_mine = lax.dynamic_slice_in_dim(grads, core * half, half, 0)
    grad_theirs = lax.dynamic_slice_in_dim(grads, (1 - core) * half, half, 0)
    grad_rows = jnp.stack([grad_mine, send(grad_theirs, SIBLING)])
    grad_rows = jnp.pad(grad_rows, ((0, 0), (0, rows_2.shape[1] - half), (0, 0)))
    grad_sibling = send(grads, SIBLING)
    part = jnp.concatenate(
        [turned_product(act_basis, query_acts), turned_product(grad_basis, query_grads)], axis=0
    )
    queries = query_acts.shape[0]
    part = jnp.pad(part, ((0, -part.shape[0] % 64), (0, 0))).reshape(4, 2, -1, queries)
    largest = largest_over(
        jnp.where(
            lax.broadcasted_iota(jnp.int32, (8, 128), 0) < 4,
            jnp.max(jnp.abs(activations)).astype(jnp.float32),
            jnp.max(jnp.abs(out_grads)).astype(jnp.float32),
        ),
        lambda x, y, z, c: (x, y, z, c + 1),
        lambda x, y, z, c: (x, y, z ^ 1, c),
        lambda x, y, z, c: (x, y, z + 2, c),
        lambda x, y, z, c: (x ^ 1, y, z, c),
        lambda x, y, z, c: (x + 2, y, z, c),
    )
    n_2 = rows_2.shape[1]
    rows_2 = jnp.concatenate([rows_2, grad_rows], axis=1)
    largest, other, sibling, grads, rows_2, grad_sibling, part = lax.optimization_barrier(
        (largest, other, sibling, grads, rows_2, grad_sibling, part)
    )
    rows_2 = round_x(rows_2)
    largest = largest_over(
        largest, lambda x, y, z, c: (x, y ^ 1, z, c), lambda x, y, z, c: (x, y + 2, z, c)
    )
    act_down, act_most = scales(largest[0, 0], tokens_total)
    grad_down, grad_most = scales(largest[4, 0], tokens_total)
    columns = [activations, sibling, other, send(other, SIBLING)]
    columns, rows_1, grads, grad_sibling, part, act_down, act_most, grad_down, grad_most = (
        lax.optimization_barrier(
            (columns, rows_1, grads, grad_sibling, part, act_down, act_most, grad_down, grad_most)
        )
    )

    width, grad_width = activations.shape[1], grads.shape[0]
    down = jnp.where(jnp.arange(width + grad_width) < width, act_down, grad_down)
    stays = y_lo == y_hi
    second, third = products(source, (2, 3), rows_1, FIRST, columns)
    grad_other = send(grads, OTHER_COLUMN)
    a = send((second * act_down).astype(HALF), Z_ALONG)
    c = send((third * act_down).astype(HALF), Z_AGAINST)
    close = products(source, (0, 1), rows_1, FIRST, columns)
    part = give(part, y_hi, OTHER_COLUMN, 1)
    grad_columns = [grads, grad_sibling, grad_other, send(grad_other, SIBLING)]
    message = (close[1] * act_down + a.astype(jnp.float32)).astype(HALF)
    message, rows_2, part = lax.optimization_barrier((message, rows_2, part))
    one = {"close": close, "down": act_down, "b": send(message, Z_ALONG), "c": c}

    second, third = products(source, (2, 3), rows_2, n_2, columns, grad_columns)
    part = scatter_x(add(*part, y_hi, 1), x)
    total = summed(one)
    messages = (
        (second * down).astype(HALF),
        (third * down).astype(HALF),
        jnp.where(stays, total[1], total[0]).astype(HALF),
    )
    messages, rows_2 = lax.optimization_barrier((messages, rows_2))
    a, c = send(messages[0], Z_ALONG), send(messages[1], Z_AGAINST)
    one = {"total": total, "n": send(messages[2], Y_PARTNER)}
    two = {"close": products(source, (0, 1), rows_2, n_2, columns, grad_columns)}
    two = {**two, "down": down, "a": a, "c": c}
    part = sum(part)
    part = (part, send(part, OTHER_COLUMN))

    message = crossing(one)
    message, two = lax.optimization_barrier((message, two))
    one["m"] = send(message, Y_MIDDLE)
    two = along(two)
    part = round_x(jnp.where(y_hi == 0, jnp.stack(part), jnp.stack(part[::-1])))

    two = across(two, stays)
    act_cov = jnp.concatenate(
        [crossed(one, stays), result(two, stays)[:, :width]], axis=0
    )
    grad_cov = result(two, stays)[:half, width : width + out_grads.shape[1]]
    part = part.reshape(-1, queries)
    split, end = act_basis.shape[1], act_basis.shape[1] + grad_basis.shape[1]
    return (mean(act_cov, act_most, tokens_total), mean(grad_cov, grad_most, tokens_total), part[:split].T, part[split:end].T)


def solution(mesh):
    return jax.shard_map(
        on_device,
        mesh=mesh,
        in_specs=(
            P("dp", "block"),
            P("dp", "block"),
            P("block", "dp"),
            P("block", "dp"),
            P(None, "block"),
            P(None, "block"),
        ),
        out_specs=(P("dp", "block"), P("dp", "block"), P(None, "dp"), P(None, "dp")),
        check_vma=False,
    )
```

```python
import functools
import itertools

import jax
import jax.numpy as jnp
from jax import lax
from jax.experimental import pallas as pl
from jax.experimental.pallas import tpu as pltpu
from jax.sharding import PartitionSpec as P

AXES = ("dp", "block")
HALF = jnp.float16


def place(x, y, z, core):
    return ((z * 2 + y % 2) * 2 + core) * 8 + x * 2 + y // 2


def pairs(move):
    out = []
    for at in itertools.product(range(4), range(4), range(4), range(2)):
        x, y, z, core = move(*at)
        out.append((place(*at), place(x % 4, y % 4, z % 4, core % 2)))
    return out


SIBLING = pairs(lambda x, y, z, c: (x, y, z, c + 1))
OTHER_COLUMN = pairs(lambda x, y, z, c: (x, y + 2, z, c))
X_DOWN = pairs(lambda x, y, z, c: (x - 1, y, z, c))
X_UP = pairs(lambda x, y, z, c: (x + 1, y, z, c))
X_FAR = pairs(lambda x, y, z, c: (x + 2, y, z, c))
Z_ALONG = pairs(lambda x, y, z, c: (x, y, z + 1 - 2 * c, c))
Z_AGAINST = pairs(lambda x, y, z, c: (x, y, z - 1 + 2 * c, c))
X_RINGS = [
    [place(x, y, z, c) for x in range(4)]
    for y, z, c in itertools.product(range(4), range(4), range(2))
]
FIRST = 304
Y_PARTNER = pairs(lambda x, y, z, c: (x, y ^ 1, z, c))
Y_ROUND = pairs(lambda x, y, z, c: (x, (2, 0, 3, 1)[y], z, c))
Y_MIDDLE = [p for p in pairs(lambda x, y, z, c: (x, (0, 2, 1, 3)[y], z, c)) if p[0] != p[1]]


def send(value, to):
    return lax.ppermute(value, AXES, to)


def turn_kernel(core, own, mine, theirs, turned):
    half = mine.shape[0]
    turned[...] = own[...].T
    mine[...] = turned[pl.ds(pl.multiple_of(core[0] * half, 16), half), :]
    theirs[...] = turned[pl.ds(pl.multiple_of((1 - core[0]) * half, 16), half), :]


def turn(own, core):
    tokens, width = own.shape
    vmem = pl.BlockSpec(memory_space=pltpu.VMEM)
    half = jax.ShapeDtypeStruct((width // 2, tokens), own.dtype)
    return pl.pallas_call(
        turn_kernel,
        out_shape=(half, half),
        in_specs=[pl.BlockSpec(memory_space=pltpu.SMEM), vmem],
        out_specs=(vmem, vmem),
        scratch_shapes=[pltpu.VMEM((width, tokens), own.dtype)],
        compiler_params=pltpu.CompilerParams(vmem_limit_bytes=24 << 20),
    )(core.reshape(1).astype(jnp.int32), own)


def product_kernel(kinds, slots, source, rows, *refs):
    count = len(slots)
    columns_of, refs = refs[: 4 * len(kinds)], refs[4 * len(kinds) :]
    outs, refs = refs[:count], refs[count:]
    *buffers, sem = refs
    block, at = pl.program_id(0), pl.program_id(1)
    start, column_waits, row_waits, work = [], ([], []), [[] for _ in slots], []
    lane = 0
    for kind, (first, turned) in enumerate(kinds):
        held, columns, landing = buffers[3 * kind : 3 * kind + 3]
        n, tokens = held.shape[1], held.shape[2] // 2
        width = columns.shape[2]
        part = [pl.ds(half * tokens, tokens) for half in (0, 1)]
        for i in (0, 1):
            for half in (0, 1):
                ref = columns_of[4 * kind + 2 * i + half]
                if turned:
                    place = landing.at[i, :, part[half]]
                else:
                    place = columns.at[i, part[half], :]
                column_waits[i].append(
                    pltpu.make_async_copy(ref, place, sem.at[kind, half, i])
                )
        for i, slot in enumerate(slots):
            for half in (0, 1):
                row_waits[i].append(
                    pltpu.make_async_copy(
                        rows.at[source[slot], half, pl.ds(first, n), :],
                        held.at[i, :, part[half]],
                        sem.at[kind, half, 2 + i],
                    )
                )
        work.append((held, columns, landing if turned else None, lane, width))
        lane += width

    @pl.when((block == 0) & (at == 0))
    def _():
        for copy in column_waits[0] + sum(row_waits, []) + column_waits[1]:
            copy.start()

    for i in (0, 1):

        @pl.when((block == i) & (at == 0))
        def _(i=i):
            for copy in column_waits[i]:
                copy.wait()
            for _, columns, landing, _, _ in work:
                if landing is not None:
                    columns[i] = landing[i].T

    for i in range(count):

        @pl.when((block == 0) & (at == i))
        def _(i=i):
            for copy in row_waits[i]:
                copy.wait()

    for i, out in enumerate(outs):

        @pl.when(at == i)
        def _(i=i, out=out):
            for held, columns, _, lane, width in work:
                out[0, :, lane : lane + width] = jnp.dot(
                    held[i], columns[block], preferred_element_type=jnp.float32
                )


def products(source, slots, rows, n, columns, grad_columns=()):
    tokens = rows.shape[3]
    dtype = rows.dtype
    count = len(slots)
    kinds, widths, buffers = [(0, False)], [columns[0].shape[1]], []
    if grad_columns:
        kinds.append((n, True))
        widths.append(grad_columns[0].shape[0])
    for (_, turned), width in zip(kinds, widths):
        buffers += [
            pltpu.VMEM((count, n, 2 * tokens), dtype),
            pltpu.VMEM((2, 2 * tokens, width), dtype),
            pltpu.VMEM((2, width, 2 * tokens) if turned else (16, 128), dtype),
        ]
    anywhere = pl.BlockSpec(memory_space=pl.ANY)
    smem = pl.BlockSpec(memory_space=pltpu.SMEM)
    return pl.pallas_call(
        functools.partial(product_kernel, kinds, slots),
        out_shape=[jax.ShapeDtypeStruct((2, n, sum(widths)), jnp.float32)] * count,
        grid=(2, count),
        in_specs=[smem] + [anywhere] * (1 + 4 * len(kinds)),
        out_specs=[pl.BlockSpec((1, n, sum(widths)), lambda block, at: (block, 0, 0))] * count,
        scratch_shapes=[*buffers, pltpu.SemaphoreType.DMA((len(kinds), 2, 2 + count))],
        compiler_params=pltpu.CompilerParams(vmem_limit_bytes=60 << 20),
        cost_estimate=pl.CostEstimate(
            flops=4 * count * n * tokens * sum(widths),
            bytes_accessed=4 * count * n * tokens,
            transcendentals=0,
        ),
    )(source, rows, *columns, *grad_columns)


def largest_over(largest, *moves):
    for move in moves:
        largest = jnp.maximum(largest, send(largest, pairs(move)))
    return largest


def scales(largest, tokens_total):
    largest = jnp.maximum(largest, 1e-18)
    most = largest * largest * tokens_total
    return 32768.0 / most, most


def mean(scaled, most, tokens_total):
    return scaled * (1.0 / (32768.0 * tokens_total)) * most


def along(p):
    b = p["close"][1] * p["down"] + p["a"].astype(jnp.float32)
    return {**p, "a": None, "b": send(b.astype(HALF), Z_ALONG)}


def summed(p):
    b, c = p["b"].astype(jnp.float32), p["c"].astype(jnp.float32)
    return p["close"][0] * p["down"] + b + c


def crossing(p):
    return (p["total"][1] + p["n"].astype(jnp.float32)).astype(HALF)


def crossed(p, stays):
    own = p["total"][0] + p["n"].astype(jnp.float32)
    return jnp.where(stays, own, p["m"].astype(jnp.float32))


def across(p, stays):
    total = summed(p)
    value = jnp.where(stays, total[1], total[0])
    n, m = send(value.astype(HALF), Y_ROUND), send(total[1].astype(HALF), Y_MIDDLE)
    return {"total": total, "n": n, "m": m}


def result(p, stays):
    other = jnp.where(stays, p["total"][0], p["m"].astype(jnp.float32))
    return p["n"].astype(jnp.float32) + other


def turned_product(basis, queries):
    return lax.dot_general(
        basis, queries, (((0,), (1,)), ((), ())), preferred_element_type=jnp.float32
    )


def give(value, bit, to, axis):
    return (value, send(lax.dynamic_slice_in_dim(value, 1 - bit, 1, axis), to))


def add(value, got, bit, axis):
    return lax.dynamic_slice_in_dim(value, bit, 1, axis) + got


def scatter_x(value, x):
    quarter = [
        lax.dynamic_index_in_dim(value[:, 0], (x + d) % 4, 0, keepdims=False) for d in range(4)
    ]
    return [quarter[0]] + [send(q, to) for q, to in zip(quarter[1:], (X_UP, X_FAR, X_DOWN))]


def round_x(rows):
    return lax.all_gather(rows, AXES, axis_index_groups=X_RINGS)


def on_device(activations, out_grads, act_basis, grad_basis, query_acts, query_grads):
    dp, block = lax.axis_index("dp"), lax.axis_index("block")
    x, y_hi, z, y_lo, core = block // 2, block % 2, dp // 4, dp // 2 % 2, dp % 2
    tokens_total = activations.shape[0] * lax.axis_size("dp")
    source = jnp.stack([(z + d * (1 - 2 * core)) % 4 for d in range(4)]).astype(jnp.int32)
    half = out_grads.shape[1] // 2

    mine, theirs = turn(activations, core)
    other = send(activations, OTHER_COLUMN)
    got = send(theirs, SIBLING)
    rows_1 = round_x(jnp.stack([mine[:FIRST], got[:FIRST]]))
    rows_2 = jnp.stack([mine[FIRST:], got[FIRST:]])
    sibling = send(activations, SIBLING)
    grads = jnp.pad(out_grads.T, ((0, -out_grads.shape[1] % 16), (0, 0)))
    grad_mine = lax.dynamic_slice_in_dim(grads, core * half, half, 0)
    grad_theirs = lax.dynamic_slice_in_dim(grads, (1 - core) * half, half, 0)
    grad_rows = jnp.stack([grad_mine, send(grad_theirs, SIBLING)])
    grad_rows = jnp.pad(grad_rows, ((0, 0), (0, rows_2.shape[1] - half), (0, 0)))
    grad_sibling = send(grads, SIBLING)
    part = jnp.concatenate(
        [turned_product(act_basis, query_acts), turned_product(grad_basis, query_grads)], axis=0
    )
    queries = query_acts.shape[0]
    part = jnp.pad(part, ((0, -part.shape[0] % 64), (0, 0))).reshape(4, 2, -1, queries)
    largest = largest_over(
        jnp.where(
            lax.broadcasted_iota(jnp.int32, (8, 128), 0) < 4,
            jnp.max(jnp.abs(activations)).astype(jnp.float32),
            jnp.max(jnp.abs(out_grads)).astype(jnp.float32),
        ),
        lambda x, y, z, c: (x, y, z, c + 1),
        lambda x, y, z, c: (x, y, z ^ 1, c),
        lambda x, y, z, c: (x, y, z + 2, c),
        lambda x, y, z, c: (x ^ 1, y, z, c),
        lambda x, y, z, c: (x + 2, y, z, c),
    )
    n_2 = rows_2.shape[1]
    rows_2 = jnp.concatenate([rows_2, grad_rows], axis=1)
    largest, other, sibling, grads, rows_2, grad_sibling, part = lax.optimization_barrier(
        (largest, other, sibling, grads, rows_2, grad_sibling, part)
    )
    rows_2 = round_x(rows_2)
    largest = largest_over(
        largest, lambda x, y, z, c: (x, y ^ 1, z, c), lambda x, y, z, c: (x, y + 2, z, c)
    )
    act_down, act_most = scales(largest[0, 0], tokens_total)
    grad_down, grad_most = scales(largest[4, 0], tokens_total)
    columns = [activations, sibling, other, send(other, SIBLING)]
    columns, rows_1, grads, grad_sibling, part, act_down, act_most, grad_down, grad_most = (
        lax.optimization_barrier(
            (columns, rows_1, grads, grad_sibling, part, act_down, act_most, grad_down, grad_most)
        )
    )

    width, grad_width = activations.shape[1], grads.shape[0]
    down = jnp.where(jnp.arange(width + grad_width) < width, act_down, grad_down)
    stays = y_lo == y_hi
    second, third = products(source, (2, 3), rows_1, FIRST, columns)
    grad_other = send(grads, OTHER_COLUMN)
    a = send((second * act_down).astype(HALF), Z_ALONG)
    c = send((third * act_down).astype(HALF), Z_AGAINST)
    close = products(source, (0, 1), rows_1, FIRST, columns)
    part = give(part, y_hi, OTHER_COLUMN, 1)
    grad_columns = [grads, grad_sibling, grad_other, send(grad_other, SIBLING)]
    message = (close[1] * act_down + a.astype(jnp.float32)).astype(HALF)
    message, rows_2, part = lax.optimization_barrier((message, rows_2, part))
    one = {"close": close, "down": act_down, "b": send(message, Z_ALONG), "c": c}

    second, third = products(source, (2, 3), rows_2, n_2, columns, grad_columns)
    part = scatter_x(add(*part, y_hi, 1), x)
    total = summed(one)
    messages = (
        (second * down).astype(HALF),
        (third * down).astype(HALF),
        jnp.where(stays, total[1], total[0]).astype(HALF),
    )
    messages, rows_2 = lax.optimization_barrier((messages, rows_2))
    a, c = send(messages[0], Z_ALONG), send(messages[1], Z_AGAINST)
    one = {"total": total, "n": send(messages[2], Y_PARTNER)}
    two = {"close": products(source, (0, 1), rows_2, n_2, columns, grad_columns)}
    two = {**two, "down": down, "a": a, "c": c}
    part = sum(part)
    part = (part, send(part, OTHER_COLUMN))

    message = crossing(one)
    message, two["close"] = lax.optimization_barrier((message, two["close"]))
    one["m"] = send(message, Y_MIDDLE)
    two = along(two)
    one, two = lax.optimization_barrier((one, two))
    part = round_x(jnp.where(y_hi == 0, jnp.stack(part), jnp.stack(part[::-1])))

    two = across(two, stays)
    act_cov = jnp.concatenate(
        [crossed(one, stays), result(two, stays)[:, :width]], axis=0
    )
    grad_cov = result(two, stays)[:half, width : width + out_grads.shape[1]]
    part = part.reshape(-1, queries)
    split, end = act_basis.shape[1], act_basis.shape[1] + grad_basis.shape[1]
    return (mean(act_cov, act_most, tokens_total), mean(grad_cov, grad_most, tokens_total), part[:split].T, part[split:end].T)


def solution(mesh):
    return jax.shard_map(
        on_device,
        mesh=mesh,
        in_specs=(
            P("dp", "block"),
            P("dp", "block"),
            P("block", "dp"),
            P("block", "dp"),
            P(None, "block"),
            P(None, "block"),
        ),
        out_specs=(P("dp", "block"), P("dp", "block"), P(None, "dp"), P(None, "dp")),
        check_vma=False,
    )
```
